32 devices in a mesh: parts: 1, batch: 16 (over z, y, core), mp: 2 (over x).
Axes of the slice: x: 2, y: 2, z: 4, core: 2. Of those that a mesh axis runs over, the one named last changes fastest.
Arguments:
- activations: bfloat16 [4096, 4096], P(('parts', 'batch'), 'mp'), may hold values from -6 to 6
- output_gradient: bfloat16 [4096, 4096], P(('parts', 'batch'), 'mp'), may hold values from -6 to 6
- levels: bfloat16 [4096, 4096], P('mp', 'batch'), may hold values from -0.09375 to 0.09375
- scales: bfloat16 [4096, 64], P('mp', 'batch'), may hold values from 0.5 to 2
- adapter_down_rows: bfloat16 [512, 4096], P(('parts', 'batch'), 'mp'), may hold values from -0.09375 to 0.09375
- adapter_up_rows: bfloat16 [512, 4096], P(('parts', 'batch'), 'mp'), may hold values from -0.09375 to 0.09375
- tenant_per_tile: int32 [32, 1], P(('parts', 'batch')), may hold values from 0 to 31
- tenant_adapter_index: int32 [32], P('parts'), may hold values from 0 to 31, each once
Outputs:
- input_gradient: bfloat16 [4096, 4096], P(('parts', 'batch'), 'mp')
- down_grads: float32 [512, 4096], P(('parts', 'batch'), 'mp')
- up_grads: float32 [512, 4096], P(('parts', 'batch'), 'mp')
The draws below stay inside these ranges and needn't reach their ends.
Inputs may be any that keep to these rules, and one draw needn't show every extreme that they name: `tenant_per_tile`: every tenant has some tile. `tenant_adapter_index`: each adapter serves exactly one tenant.
All inputs are finite; a program needn't handle non-finite values.
Results may differ from the reference program's by a relative error of at most 0.009.
Values may be sent and summed in bfloat16 or wider, within the bound.
A program may use at most 128 MiB of HBM per device.

```python
import math
import jax
import jax.numpy as jnp
from jax import lax

INPUT_FEATURES = 4096
OUTPUT_FEATURES = 4096
ADAPTER_RANK = 16
ADAPTER_TOTAL = 32
TILE = 128
QB = 64
TOKEN_TOTAL = 4096
TILES = 32


def shard_levels(stream_key, shape, pieces, low, largest):
    factor_of, own = 1.0, jax.random.fold_in(stream_key, 6)
    for dim, parts in pieces:
        draws = jnp.exp(jax.random.uniform(jax.random.fold_in(own, dim), (parts,), jnp.float32, low / len(pieces), largest / len(pieces)))
        factor_of = factor_of * jnp.repeat(draws, shape[dim] // parts).reshape([-1 if axis == dim else 1 for axis in range(len(shape))])
    return factor_of


def distinct(own_key, rows, amount, top, lift):
    order = jax.random.permutation(jax.random.fold_in(own_key, 1), amount)
    pull = order
    for power in range(3):
        pull = pull * pull // amount
    pull = pull * lift // amount
    chance = jax.random.randint(jax.random.fold_in(own_key, 2), (rows, amount), 0, 4096) + pull
    holders = jax.random.permutation(jax.random.fold_in(own_key, 3), rows)[jnp.arange(amount) % rows]
    chance = jnp.where(jnp.arange(rows)[:, None] == holders[None, :], 1 << 14, chance)
    score = chance * amount + jnp.arange(amount)
    return lax.top_k(score.astype(jnp.int32), top)[1].astype(jnp.int32)


def centred(stream_key, shape, scale, limit, shards=(), held_as=jnp.bfloat16):
    array = jax.random.normal(stream_key, shape, jnp.float32) * scale
    if len(shards) > 0:
        array = shard_levels(stream_key, shape, shards, -0.22, 0.18) * array
    return jnp.clip(array, min=-limit, max=limit).astype(held_as)


def setup_inputs(seed: int = 0, part: int = 0) -> dict:
    keys = jax.random.split(jax.random.key(seed), 9)
    part_splits = jax.random.split(jax.random.fold_in(keys[8], part), 9)
    activations = centred(part_splits[0], (TOKEN_TOTAL, INPUT_FEATURES), 1.0, 6.0, ((0, 16), (1, 2)))
    output_gradient = centred(part_splits[1], (TOKEN_TOTAL, OUTPUT_FEATURES), 1.0, 6.0, ((0, 16), (1, 2)))
    levels = centred(keys[2], (INPUT_FEATURES, OUTPUT_FEATURES), OUTPUT_FEATURES ** -0.5, 0.09375, ((0, 2), (1, 16)))
    scales = jnp.clip(jnp.exp(math.log(2.0) - 1.3862944 * jax.random.uniform(keys[3], (INPUT_FEATURES, OUTPUT_FEATURES // QB), jnp.float32) ** shard_levels(keys[3], (INPUT_FEATURES, OUTPUT_FEATURES // QB), ((0, 2), (1, 16)), -0.2, 0.2)), 0.5, 2.0).astype(jnp.bfloat16)
    adapter_down_rows = centred(part_splits[4], (ADAPTER_TOTAL * ADAPTER_RANK, INPUT_FEATURES), INPUT_FEATURES ** -0.5, 0.09375, ((0, 16), (1, 2)))
    adapter_up_rows = centred(part_splits[5], (ADAPTER_TOTAL * ADAPTER_RANK, OUTPUT_FEATURES), OUTPUT_FEATURES ** -0.5, 0.09375, ((0, 16), (1, 2)))
    tenant_per_tile = distinct(part_splits[6], TILES, ADAPTER_TOTAL, 1, 512)
    tenant_adapter_index = jax.random.permutation(part_splits[7], ADAPTER_TOTAL).astype(jnp.int32)
    return dict(activations=activations, output_gradient=output_gradient, levels=levels, scales=scales, adapter_down_rows=adapter_down_rows, adapter_up_rows=adapter_up_rows, tenant_per_tile=tenant_per_tile, tenant_adapter_index=tenant_adapter_index)


def reference(activations, output_gradient, levels, scales, adapter_down_rows, adapter_up_rows, tenant_per_tile, tenant_adapter_index):
    weight = (levels.astype(jnp.float32) * jnp.repeat(scales.astype(jnp.float32), QB, axis=1)).astype(jnp.bfloat16)
    base_product = jnp.dot(output_gradient, weight.T, preferred_element_type=jnp.float32)
    tile_owner = tenant_adapter_index[tenant_per_tile[:, 0]].astype(jnp.int32)
    row_owner = jnp.repeat(tile_owner, TILE)
    row_hot = row_owner[:, None] == jnp.arange(ADAPTER_TOTAL, dtype=jnp.int32)[None, :]
    onehot_float = row_hot.astype(jnp.float32)
    complete_hidden = jnp.dot(activations, adapter_down_rows.T, preferred_element_type=jnp.float32).reshape(TOKEN_TOTAL, ADAPTER_TOTAL, ADAPTER_RANK)
    complete_coefficients = jnp.dot(output_gradient, adapter_up_rows.T, preferred_element_type=jnp.float32).reshape(TOKEN_TOTAL, ADAPTER_TOTAL, ADAPTER_RANK)
    adapter_hidden = jnp.sum(complete_hidden * onehot_float[:, :, None], axis=1)
    adapter_coefficients = jnp.sum(complete_coefficients * onehot_float[:, :, None], axis=1)
    hidden_narrow16 = adapter_hidden.astype(jnp.bfloat16)
    coefficients16 = adapter_coefficients.astype(jnp.bfloat16)
    hot16 = row_hot.astype(jnp.bfloat16)
    coefficients_widened = (hot16[:, :, None] * coefficients16[:, None, :]).reshape(TOKEN_TOTAL, ADAPTER_TOTAL * ADAPTER_RANK)
    hidden_wide = (hot16[:, :, None] * hidden_narrow16[:, None, :]).reshape(TOKEN_TOTAL, ADAPTER_TOTAL * ADAPTER_RANK)
    adapter_contribution = (2.0 * jnp.dot(coefficients_widened, adapter_down_rows, preferred_element_type=jnp.float32)).astype(jnp.bfloat16)
    input_gradient = (base_product + adapter_contribution.astype(jnp.float32)).astype(jnp.bfloat16)
    down_grads = 2.0 * jnp.dot(coefficients_widened.T, activations, preferred_element_type=jnp.float32)
    up_grads = 2.0 * jnp.dot(hidden_wide.T, output_gradient, preferred_element_type=jnp.float32)
    return input_gradient, down_grads, up_grads
```

```python
import jax
import jax.numpy as jnp
from jax import lax
from jax.experimental import pallas as pl
from jax.experimental.pallas import tpu as pltpu
from jax.sharding import PartitionSpec as P

ADAPTER_RANK = 16
QB = 64


def contract(left, right, left_dim, right_dim):
    return lax.dot_general(
        left, right, (((left_dim,), (right_dim,)), ((), ())), preferred_element_type=jnp.float32
    )


def dequantize(level_cols, scale_cols):
    return (
        level_cols.astype(jnp.float32) * jnp.repeat(scale_cols.astype(jnp.float32), QB, axis=1)
    ).astype(jnp.bfloat16)


def body(
    activations,
    output_gradient,
    levels,
    scales,
    adapter_down_rows,
    adapter_up_rows,
    tenant_per_tile,
    tenant_adapter_index,
):
    rows_dev, inner_local = activations.shape
    tiles_here = tenant_per_tile.shape[0]
    tile_rows = rows_dev // tiles_here
    adapter_count = tenant_adapter_index.shape[0]
    full_grads = lax.all_gather(output_gradient, "mp", axis=1, tiled=True)
    local_weight = dequantize(levels, scales)
    base_total = contract(
        full_grads, lax.all_gather(local_weight, "batch", axis=1, tiled=True), 1, 1
    )
    stacked_down_factors, all_up = (
        lax.all_gather(adapter_down_rows, "batch", axis=0, tiled=True),
        lax.all_gather(adapter_up_rows, "batch", axis=0, tiled=True),
    )
    tenants = tenant_per_tile[:, 0]
    adapter_ids = jnp.arange(adapter_count, dtype=jnp.int32)
    tenant_match = (tenants[:, None] == adapter_ids[None, :]).astype(jnp.int32)
    owner_of = jnp.sum(tenant_match * tenant_adapter_index[None, :], axis=1)
    tile_hot = owner_of[:, None] == adapter_ids[None, :]
    row_hot = jnp.broadcast_to(
        tile_hot[:, None, :], (tiles_here, tile_rows, adapter_count)
    ).reshape(rows_dev, adapter_count)
    onehot_float = row_hot.astype(jnp.float32)
    wide_hidden = contract(activations, stacked_down_factors, 1, 1).reshape(
        rows_dev, adapter_count, ADAPTER_RANK
    )
    wide_coeffs = contract(output_gradient, all_up, 1, 1).reshape(
        rows_dev, adapter_count, ADAPTER_RANK
    )
    hidden_share = jnp.sum(wide_hidden * onehot_float[:, :, None], axis=1)
    coefficient_share = jnp.sum(wide_coeffs * onehot_float[:, :, None], axis=1)
    adapter_hidden, adapter_coefficients = (
        lax.psum(hidden_share.astype(jnp.bfloat16), "mp").astype(jnp.float32),
        lax.psum(coefficient_share.astype(jnp.bfloat16), "mp").astype(jnp.float32),
    )
    hidden_narrow16 = adapter_hidden.astype(jnp.bfloat16)
    coefficients16 = adapter_coefficients.astype(jnp.bfloat16)
    hot16 = row_hot.astype(jnp.bfloat16)
    coefficients_widened = (hot16[:, :, None] * coefficients16[:, None, :]).reshape(
        rows_dev, adapter_count * ADAPTER_RANK
    )
    hidden_wide = (hot16[:, :, None] * hidden_narrow16[:, None, :]).reshape(
        rows_dev, adapter_count * ADAPTER_RANK
    )
    adapter_contribution = (
        2.0
        * jnp.dot(coefficients_widened, stacked_down_factors, preferred_element_type=jnp.float32)
    ).astype(jnp.bfloat16)
    down_terms = 2.0 * contract(coefficients_widened, activations, 0, 0)
    up_terms = 2.0 * contract(hidden_wide, output_gradient, 0, 0)
    down_grads, up_grads = (
        lax.psum_scatter(down_terms, "batch", scatter_dimension=0, tiled=True),
        lax.psum_scatter(up_terms, "batch", scatter_dimension=0, tiled=True),
    )
    input_gradient = (base_total + adapter_contribution.astype(jnp.float32)).astype(jnp.bfloat16)
    return (input_gradient, down_grads, up_grads)

DEPTH, PIECES, UP, DOWN, ACROSS, SIBLING = 4, 2, 0, 1, 2, 3
CHUNK = 256


def fused_kernel(
    spots, act, grad, weight, down_own, up_own,
    out, terms,
    wbuf, fac, gfull, acc, share, theirs,
    w_recv, w_send, f_recv, f_send, t_recv, t_send, x_recv, x_send,
):
    slots, pieces, piece_rows, width = wbuf.shape
    tiles = spots.shape[0]
    me, half = lax.axis_index("batch"), lax.axis_index("mp")
    z, y, core = me // 4, (me // 2) % 2, me % 2
    place = {
        UP: {"batch": me + 4},
        DOWN: {"batch": me - 4},
        ACROSS: {"batch": z * 4 + (1 - y) * 2 + core},
        SIBLING: {"batch": z * 4 + y * 2 + 1 - core},
    }
    partner = {"mp": 1 - half}
    not_top, not_bottom = z < DEPTH - 1, z > 0

    inner, upper = z * (3 - z) // 2, z // 2

    def near(k):
        v = inner + k - 2 * inner * k if k < 2 else k
        return v + upper * (3 - 2 * v)

    def slot(k, plane, column):
        yy = y if plane == 0 else 1 - y
        cc = core if column == 0 else 1 - core
        return near(k) * 4 + yy * 2 + cc

    barrier = pltpu.get_barrier_semaphore()
    for way, there in ((UP, not_top), (DOWN, not_bottom)):
        @pl.when(there)
        def _(way=way):
            pl.semaphore_signal(barrier, inc=1, device_id=place[way], device_id_type=pl.DeviceIdType.MESH)
    for to in (place[ACROSS], place[SIBLING], partner):
        pl.semaphore_signal(barrier, inc=1, device_id=to, device_id_type=pl.DeviceIdType.MESH)
    pl.semaphore_wait(barrier, 4 + inner)

    started = []

    def copy(src, dst, send, recv, to):
        return pltpu.make_async_remote_copy(
            src_ref=src, dst_ref=dst, send_sem=send, recv_sem=recv,
            device_id=to, device_id_type=pl.DeviceIdType.MESH,
        )

    def push(src, dst, send, recv, way, when=None):
        moved = copy(src, dst, send.at[way], recv, place[way])
        started.append((moved, when))
        if when is None:
            moved.start()
        else:
            pl.when(when)(moved.start)

    def spread(src, dst, send, recv, k, across):
        from_z = near(k)
        push(src, dst, send, recv, UP, jnp.logical_and(from_z <= z, not_top))
        push(src, dst, send, recv, DOWN, jnp.logical_and(from_z >= z, not_bottom))
        if across:
            push(src, dst, send, recv, ACROSS)
        push(src, dst, send, recv, SIBLING)

    def landed(ref, recv):
        copy(ref, ref, x_send.at[0], recv, partner).wait_recv()

    def weight_on(k, plane):
        s = slot(k, plane, 0)
        for p in range(pieces):
            dst = wbuf.at[s, p]
            src = weight.at[p] if k == 0 and plane == 0 else dst
            if src is dst:
                landed(dst, w_recv.at[s, p])
            if plane == 0:
                spread(src, dst, w_send.at[k, p], w_recv.at[s, p], k, True)
            else:
                push(src, dst, w_send.at[DEPTH + k, p], w_recv.at[s, p], SIBLING)

    def weight_in(k, plane):
        s = slot(k, plane, 1)
        for p in range(pieces):
            landed(wbuf.at[s, p], w_recv.at[s, p])

    def multiply(k, plane, column):
        s = slot(k, plane, column)
        per_half = gfull.shape[2] // width
        cols = pl.ds(pl.multiple_of((s % per_half) * width, width), width)
        own = k == 0 and plane == 0 and column == 0
        per_piece = piece_rows // CHUNK

        @pl.loop(0, pieces * per_piece)
        def _(j):
            rows = pl.ds(pl.multiple_of((j % per_piece) * CHUNK, CHUNK), CHUNK)
            block = weight[j // per_piece, rows, :] if own else wbuf[s, j // per_piece, rows, :]
            acc[j] += contract(gfull[s // per_half, :, cols], block, 1, 1)

    def factor_on(k, plane):
        s = slot(k, plane, 0)
        if k or plane:
            landed(fac.at[s], f_recv.at[s])
        spread(fac.at[s], fac.at[s], f_send.at[plane * DEPTH + k], f_recv.at[s], k, k == 0 and plane == 0)

    def terms_on(k, plane):
        s = slot(k, plane, 0)
        if k or plane:
            landed(terms.at[s], t_recv.at[s])
        if plane == 0:
            spread(terms.at[s], terms.at[s], t_send.at[k], t_recv.at[s], k, True)
        else:
            push(terms.at[s], terms.at[s], t_send.at[DEPTH + k], t_recv.at[s], SIBLING)

    rank = down_own.shape[1]
    for sub in range(down_own.shape[0]):
        fac[me, 0, sub] = down_own[sub]
        fac[me, 1, sub] = up_own[sub]
    factor_on(0, 0)
    weight_on(0, 0)
    cross = copy(grad, gfull.at[half], x_send.at[0], x_recv.at[0], partner)
    cross.start()
    gfull[half] = grad[...]
    share[...] = jnp.zeros_like(share)

    factor_on(0, 1)
    for k in range(1, DEPTH):
        factor_on(k, 0)
        factor_on(k, 1)
    weight_on(1, 0)
    for k in range(DEPTH):
        for plane in range(2):
            s = slot(k, plane, 1)
            landed(fac.at[s], f_recv.at[s])

    tile_rows = act.shape[0] // tiles
    for t in range(tiles):
        rows = pl.ds(t * tile_rows, tile_rows)
        where, sub = spots[t, 0], spots[t, 1]
        share[0, rows, :rank] = contract(act[rows, :], fac[where, 0, sub], 1, 1)
        share[1, rows, :rank] = contract(grad[rows, :], fac[where, 1, sub], 1, 1)
    swap = copy(share, theirs, x_send.at[1], x_recv.at[1], partner)
    swap.start()
    weight_on(2, 0)
    landed(theirs, x_recv.at[1])
    for t in range(tiles):
        rows = pl.ds(t * tile_rows, tile_rows)
        where, sub = spots[t, 0], spots[t, 1]
        hidden = share[0, rows, :] + theirs[0, rows, :]
        coeffs = share[1, rows, :] + theirs[1, rows, :]
        factor = fac[where, 0, sub]
        coeffs16 = coeffs[:, :rank].astype(jnp.bfloat16)
        lora = (2.0 * contract(coeffs16, factor, 1, 0)).astype(jnp.bfloat16).astype(jnp.float32)
        for j in range(acc.shape[0]):
            acc[j, rows, :] = lora[:, j * CHUNK : (j + 1) * CHUNK]
        turned = jnp.transpose(coeffs)[:rank].astype(jnp.bfloat16)
        terms[me, 0, t] = (2.0 * contract(turned, act[rows, :], 1, 0)).astype(jnp.bfloat16)
        turned = jnp.transpose(hidden)[:rank].astype(jnp.bfloat16)
        terms[me, 1, t] = (2.0 * contract(turned, grad[rows, :], 1, 0)).astype(jnp.bfloat16)
    terms_on(0, 0)

    landed(gfull.at[1 - half], x_recv.at[0])
    multiply(0, 0, 0)
    multiply(1, 0, 0)
    multiply(2, 0, 0)
    weight_on(0, 1)
    weight_on(1, 1)
    weight_on(3, 0)
    terms_on(1, 0)
    multiply(3, 0, 0)
    weight_in(0, 0)
    multiply(0, 0, 1)
    multiply(0, 1, 0)
    multiply(1, 1, 0)
    weight_in(1, 0)
    multiply(1, 0, 1)
    weight_on(2, 1)
    terms_on(2, 0)
    multiply(2, 1, 0)
    weight_in(0, 1)
    multiply(0, 1, 1)
    weight_in(1, 1)
    multiply(1, 1, 1)
    weight_in(2, 0)
    multiply(2, 0, 1)
    terms_on(3, 0)
    terms_on(0, 1)
    terms_on(1, 1)
    weight_in(3, 0)
    multiply(3, 0, 1)
    weight_in(2, 1)
    multiply(2, 1, 1)
    weight_on(3, 1)
    terms_on(2, 1)
    multiply(3, 1, 0)
    terms_on(3, 1)
    weight_in(3, 1)
    multiply(3, 1, 1)
    for j in range(acc.shape[0]):
        out[:, j * CHUNK : (j + 1) * CHUNK] = acc[j].astype(jnp.bfloat16)
    for k in range(DEPTH):
        for plane in range(2):
            s = slot(k, plane, 1)
            landed(terms.at[s], t_recv.at[s])
    cross.wait_send()
    swap.wait_send()
    for moved, when in started:
        if when is None:
            moved.wait_send()
        else:
            pl.when(when)(moved.wait_send)


def fused_body(
    activations,
    output_gradient,
    levels,
    scales,
    adapter_down_rows,
    adapter_up_rows,
    tenant_per_tile,
    tenant_adapter_index,
):
    rows_dev, inner_local = activations.shape
    in_rows, out_cols = levels.shape
    tiles_here = tenant_per_tile.shape[0]
    held = adapter_down_rows.shape[0] // ADAPTER_RANK
    slots = lax.axis_size("batch")
    adapter_ids = jnp.arange(tenant_adapter_index.shape[0], dtype=jnp.int32)

    def owners(tenants):
        match = (tenants[:, None] == adapter_ids[None, :]).astype(jnp.int32)
        return jnp.sum(match * tenant_adapter_index[None, :], axis=1)

    mine = owners(tenant_per_tile[:, 0])
    spots = jnp.stack([mine // held, mine % held], axis=1)
    everyone = lax.all_gather(tenant_per_tile, "batch", axis=0, tiled=True)
    weight = dequantize(levels, scales).reshape(PIECES, in_rows // PIECES, out_cols)
    factor_shape = (held, ADAPTER_RANK, inner_local)
    vmem = pl.BlockSpec(memory_space=pltpu.VMEM)
    dma = pltpu.SemaphoreType.DMA
    bf16, f32 = jnp.bfloat16, jnp.float32
    out, terms = pl.pallas_call(
        fused_kernel,
        out_shape=(
            jax.ShapeDtypeStruct((rows_dev, in_rows), bf16),
            jax.ShapeDtypeStruct((slots, 2, tiles_here, ADAPTER_RANK, inner_local), bf16),
        ),
        in_specs=[pl.BlockSpec(memory_space=pltpu.SMEM)] + [vmem] * 5,
        out_specs=(vmem, vmem),
        scratch_shapes=[
            pltpu.VMEM((slots,) + weight.shape, bf16),
            pltpu.VMEM((slots, 2) + factor_shape, bf16),
            pltpu.VMEM((2, rows_dev, inner_local), bf16),
            pltpu.VMEM((in_rows // CHUNK, rows_dev, CHUNK), f32),
            pltpu.VMEM((2, rows_dev, 128), f32),
            pltpu.VMEM((2, rows_dev, 128), f32),
            dma((slots, PIECES)),
            dma((2 * DEPTH, PIECES, 4)),
            dma((slots,)),
            dma((2 * DEPTH, 4)),
            dma((slots,)),
            dma((2 * DEPTH, 4)),
            dma((2,)),
            dma((2,)),
        ],
        compiler_params=pltpu.CompilerParams(
            collective_id=0, has_side_effects=True, vmem_limit_bytes=52 * 2**20
        ),
        cost_estimate=pl.CostEstimate(
            flops=2 * rows_dev * in_rows * out_cols * slots,
            bytes_accessed=2**27,
            transcendentals=0,
        ),
    )(
        spots,
        activations,
        output_gradient,
        weight,
        adapter_down_rows.reshape(factor_shape),
        adapter_up_rows.reshape(factor_shape),
    )
    row_of = jnp.repeat(owners(everyone[:, 0]), ADAPTER_RANK) * ADAPTER_RANK + jnp.tile(
        jnp.arange(ADAPTER_RANK, dtype=jnp.int32), everyone.shape[0]
    )
    first = lax.axis_index("batch") * held * ADAPTER_RANK
    own_rows = first + jnp.arange(held * ADAPTER_RANK, dtype=jnp.int32)
    pick = (own_rows[:, None] == row_of[None, :]).astype(bf16)
    down_grads = contract(pick, terms[:, 0].reshape(-1, inner_local), 1, 0)
    up_grads = contract(pick, terms[:, 1].reshape(-1, inner_local), 1, 0)
    return out, down_grads, up_grads


def solution(mesh):
    in_specs = (
        P(("parts", "batch"), "mp"),
        P(("parts", "batch"), "mp"),
        P("mp", "batch"),
        P("mp", "batch"),
        P(("parts", "batch"), "mp"),
        P(("parts", "batch"), "mp"),
        P(("parts", "batch"), None),
        P("parts"),
    )
    out_specs = (
        P(("parts", "batch"), "mp"),
        P(("parts", "batch"), "mp"),
        P(("parts", "batch"), "mp"),
    )
    fused = mesh.shape["batch"] == 16 and mesh.shape["mp"] == 2 and mesh.shape["parts"] == 1
    chosen = fused_body if fused else body
    return jax.shard_map(chosen, mesh=mesh, in_specs=in_specs, out_specs=out_specs, check_vma=False)
```

```python
import jax
import jax.numpy as jnp
from jax import lax
from jax.experimental import pallas as pl
from jax.experimental.pallas import tpu as pltpu
from jax.sharding import PartitionSpec as P

ADAPTER_RANK = 16
QB = 64


def contract(left, right, left_dim, right_dim):
    return lax.dot_general(
        left, right, (((left_dim,), (right_dim,)), ((), ())), preferred_element_type=jnp.float32
    )


def dequantize(level_cols, scale_cols):
    return (
        level_cols.astype(jnp.float32) * jnp.repeat(scale_cols.astype(jnp.float32), QB, axis=1)
    ).astype(jnp.bfloat16)


def body(
    activations,
    output_gradient,
    levels,
    scales,
    adapter_down_rows,
    adapter_up_rows,
    tenant_per_tile,
    tenant_adapter_index,
):
    rows_dev, inner_local = activations.shape
    tiles_here = tenant_per_tile.shape[0]
    tile_rows = rows_dev // tiles_here
    adapter_count = tenant_adapter_index.shape[0]
    full_grads = lax.all_gather(output_gradient, "mp", axis=1, tiled=True)
    local_weight = dequantize(levels, scales)
    base_total = contract(
        full_grads, lax.all_gather(local_weight, "batch", axis=1, tiled=True), 1, 1
    )
    stacked_down_factors, all_up = (
        lax.all_gather(adapter_down_rows, "batch", axis=0, tiled=True),
        lax.all_gather(adapter_up_rows, "batch", axis=0, tiled=True),
    )
    tenants = tenant_per_tile[:, 0]
    adapter_ids = jnp.arange(adapter_count, dtype=jnp.int32)
    tenant_match = (tenants[:, None] == adapter_ids[None, :]).astype(jnp.int32)
    owner_of = jnp.sum(tenant_match * tenant_adapter_index[None, :], axis=1)
    tile_hot = owner_of[:, None] == adapter_ids[None, :]
    row_hot = jnp.broadcast_to(
        tile_hot[:, None, :], (tiles_here, tile_rows, adapter_count)
    ).reshape(rows_dev, adapter_count)
    onehot_float = row_hot.astype(jnp.float32)
    wide_hidden = contract(activations, stacked_down_factors, 1, 1).reshape(
        rows_dev, adapter_count, ADAPTER_RANK
    )
    wide_coeffs = contract(output_gradient, all_up, 1, 1).reshape(
        rows_dev, adapter_count, ADAPTER_RANK
    )
    hidden_share = jnp.sum(wide_hidden * onehot_float[:, :, None], axis=1)
    coefficient_share = jnp.sum(wide_coeffs * onehot_float[:, :, None], axis=1)
    adapter_hidden, adapter_coefficients = (
        lax.psum(hidden_share.astype(jnp.bfloat16), "mp").astype(jnp.float32),
        lax.psum(coefficient_share.astype(jnp.bfloat16), "mp").astype(jnp.float32),
    )
    hidden_narrow16 = adapter_hidden.astype(jnp.bfloat16)
    coefficients16 = adapter_coefficients.astype(jnp.bfloat16)
    hot16 = row_hot.astype(jnp.bfloat16)
    coefficients_widened = (hot16[:, :, None] * coefficients16[:, None, :]).reshape(
        rows_dev, adapter_count * ADAPTER_RANK
    )
    hidden_wide = (hot16[:, :, None] * hidden_narrow16[:, None, :]).reshape(
        rows_dev, adapter_count * ADAPTER_RANK
    )
    adapter_contribution = (
        2.0
        * jnp.dot(coefficients_widened, stacked_down_factors, preferred_element_type=jnp.float32)
    ).astype(jnp.bfloat16)
    down_terms = 2.0 * contract(coefficients_widened, activations, 0, 0)
    up_terms = 2.0 * contract(hidden_wide, output_gradient, 0, 0)
    down_grads, up_grads = (
        lax.psum_scatter(down_terms, "batch", scatter_dimension=0, tiled=True),
        lax.psum_scatter(up_terms, "batch", scatter_dimension=0, tiled=True),
    )
    input_gradient = (base_total + adapter_contribution.astype(jnp.float32)).astype(jnp.bfloat16)
    return (input_gradient, down_grads, up_grads)

DEPTH, PIECES, UP, DOWN, ACROSS, SIBLING = 4, 2, 0, 1, 2, 3
CHUNK = 256


def fused_kernel(
    spots, act, grad, levels, scales_t, down_own, up_own, tag_own,
    out, down_grads, up_grads,
    weight, terms, tags, wbuf, fac, gfull, acc, share, theirs,
    w_recv, w_send, f_recv, f_send, g_recv, g_send, t_recv, t_send, x_recv, x_send,
):
    slots, pieces, piece_rows, width = wbuf.shape
    tiles = spots.shape[0]
    me, half = lax.axis_index("batch"), lax.axis_index("mp")
    z, y, core = me // 4, (me // 2) % 2, me % 2
    place = {
        UP: {"batch": me + 4},
        DOWN: {"batch": me - 4},
        ACROSS: {"batch": z * 4 + (1 - y) * 2 + core},
        SIBLING: {"batch": z * 4 + y * 2 + 1 - core},
    }
    partner = {"mp": 1 - half}
    not_top, not_bottom = z < DEPTH - 1, z > 0

    inner, upper = z * (3 - z) // 2, z // 2

    def near(k):
        v = inner + k - 2 * inner * k if k < 2 else k
        return v + upper * (3 - 2 * v)

    def slot(k, plane, column):
        yy = y if plane == 0 else 1 - y
        cc = core if column == 0 else 1 - core
        return near(k) * 4 + yy * 2 + cc

    barrier = pltpu.get_barrier_semaphore()
    for way, there in ((UP, not_top), (DOWN, not_bottom)):
        @pl.when(there)
        def _(way=way):
            pl.semaphore_signal(barrier, inc=1, device_id=place[way], device_id_type=pl.DeviceIdType.MESH)
    for to in (place[ACROSS], place[SIBLING], partner):
        pl.semaphore_signal(barrier, inc=1, device_id=to, device_id_type=pl.DeviceIdType.MESH)
    pl.semaphore_wait(barrier, 4 + inner)

    started = []

    def copy(src, dst, send, recv, to):
        return pltpu.make_async_remote_copy(
            src_ref=src, dst_ref=dst, send_sem=send, recv_sem=recv,
            device_id=to, device_id_type=pl.DeviceIdType.MESH,
        )

    def push(src, dst, send, recv, way, when=None):
        moved = copy(src, dst, send.at[way], recv, place[way])
        started.append((moved, when))
        if when is None:
            moved.start()
        else:
            pl.when(when)(moved.start)

    def along(src, dst, send, recv, k):
        from_z = near(k)
        push(src, dst, send, recv, UP, jnp.logical_and(from_z <= z, not_top))
        push(src, dst, send, recv, DOWN, jnp.logical_and(from_z >= z, not_bottom))

    def landed(ref, recv):
        copy(ref, ref, x_send.at[0], recv, partner).wait_recv()

    def z_first(ref, own, send, recv, k, plane):
        if k or plane:
            landed(ref, recv)
        src = own if k == 0 and plane == 0 else ref
        if plane == 0:
            along(src, ref, send, recv, k)
            push(src, ref, send, recv, ACROSS)
        push(src, ref, send, recv, SIBLING)

    def y_first(ref, send, recv, k, plane):
        if k or plane:
            landed(ref, recv)
        if k == 0 and plane == 0:
            push(ref, ref, send, recv, ACROSS)
        along(ref, ref, send, recv, k)
        push(ref, ref, send, recv, SIBLING)

    def weight_on(k, plane, p):
        s = slot(k, plane, 0)
        z_first(wbuf.at[s, p], weight.at[p], w_send.at[plane * DEPTH + k, p], w_recv.at[s, p], k, plane)

    def weight_in(k, plane):
        s = slot(k, plane, 1)
        for p in range(pieces):
            landed(wbuf.at[s, p], w_recv.at[s, p])

    def multiply(k, plane, column):
        s = slot(k, plane, column)
        per_half = gfull.shape[2] // width
        cols = pl.ds(pl.multiple_of((s % per_half) * width, width), width)
        own = k == 0 and plane == 0 and column == 0
        per_piece = piece_rows // CHUNK

        @pl.loop(0, pieces * per_piece)
        def _(j):
            rows = pl.ds(pl.multiple_of((j % per_piece) * CHUNK, CHUNK), CHUNK)
            block = weight[j // per_piece, rows, :] if own else wbuf[s, j // per_piece, rows, :]
            acc[j] += contract(gfull[s // per_half, :, cols], block, 1, 1)

    def factor_on(k, plane):
        s = slot(k, plane, 0)
        z_first(fac.at[s], fac.at[s], f_send.at[plane * DEPTH + k], f_recv.at[s], k, plane)
        z_first(tags.at[s], tags.at[s], g_send.at[plane * DEPTH + k], g_recv.at[s], k, plane)

    def terms_on(k, plane):
        s = slot(k, plane, 0)
        y_first(terms.at[s], t_send.at[plane * DEPTH + k], t_recv.at[s], k, plane)

    rank = down_own.shape[1]
    for sub in range(down_own.shape[0]):
        fac[me, 0, sub] = down_own[sub]
        fac[me, 1, sub] = up_own[sub]
    tags[me] = tag_own[...]
    factor_on(0, 0)
    cross = copy(grad, gfull.at[half], x_send.at[0], x_recv.at[0], partner)
    cross.start()

    groups = scales_t.shape[0]
    spread = (
        lax.broadcasted_iota(jnp.int32, (groups, width), 0)
        == lax.broadcasted_iota(jnp.int32, (groups, width), 1) // QB
    ).astype(jnp.bfloat16)

    @pl.loop(0, pieces * piece_rows // CHUNK)
    def _(j):
        rows = pl.ds(pl.multiple_of(j * CHUNK, CHUNK), CHUNK)
        inside = pl.ds(pl.multiple_of((j * CHUNK) % piece_rows, CHUNK), CHUNK)
        factor = contract(scales_t[:, rows], spread, 0, 0)
        weight[j * CHUNK // piece_rows, inside, :] = (
            levels[rows, :].astype(jnp.float32) * factor
        ).astype(jnp.bfloat16)

    gfull[half] = grad[...]
    share[...] = jnp.zeros_like(share)
    factor_on(1, 0)
    factor_on(2, 0)
    weight_on(0, 0, 0)
    factor_on(3, 0)
    weight_on(0, 0, 1)
    weight_on(1, 0, 0)
    weight_on(1, 0, 1)
    for k in range(DEPTH):
        factor_on(k, 1)
    for k in range(DEPTH):
        for plane in range(2):
            s = slot(k, plane, 1)
            landed(fac.at[s], f_recv.at[s])
            landed(tags.at[s], g_recv.at[s])

    tile_rows = act.shape[0] // tiles
    for t in range(tiles):
        rows = pl.ds(t * tile_rows, tile_rows)
        where, sub = spots[t, 0], spots[t, 1]
        share[0, rows, :rank] = contract(act[rows, :], fac[where, 0, sub], 1, 1)
        share[1, rows, :rank] = contract(grad[rows, :], fac[where, 1, sub], 1, 1)
    swap = copy(share, theirs, x_send.at[1], x_recv.at[1], partner)
    swap.start()
    weight_on(2, 0, 0)
    landed(theirs, x_recv.at[1])
    for t in range(tiles):
        rows = pl.ds(t * tile_rows, tile_rows)
        where, sub = spots[t, 0], spots[t, 1]
        hidden = share[0, rows, :] + theirs[0, rows, :]
        coeffs = share[1, rows, :] + theirs[1, rows, :]
        factor = fac[where, 0, sub]
        coeffs16 = coeffs[:, :rank].astype(jnp.bfloat16)
        lora = (2.0 * contract(coeffs16, factor, 1, 0)).astype(jnp.bfloat16).astype(jnp.float32)
        for j in range(acc.shape[0]):
            acc[j, rows, :] = lora[:, j * CHUNK : (j + 1) * CHUNK]
        turned = jnp.transpose(coeffs)[:rank].astype(jnp.bfloat16)
        terms[me, 0, t] = (2.0 * contract(turned, act[rows, :], 1, 0)).astype(jnp.bfloat16)
        turned = jnp.transpose(hidden)[:rank].astype(jnp.bfloat16)
        terms[me, 1, t] = (2.0 * contract(turned, grad[rows, :], 1, 0)).astype(jnp.bfloat16)
    terms_on(0, 0)
    weight_on(2, 0, 1)
    landed(gfull.at[1 - half], x_recv.at[0])
    multiply(0, 0, 0)
    weight_on(3, 0, 0)
    multiply(1, 0, 0)
    weight_on(3, 0, 1)
    terms_on(0, 1)
    terms_on(1, 0)
    terms_on(1, 1)
    weight_on(0, 1, 0)
    weight_on(0, 1, 1)
    terms_on(2, 0)
    multiply(2, 0, 0)
    terms_on(2, 1)
    weight_on(1, 1, 0)
    weight_on(1, 1, 1)
    multiply(3, 0, 0)
    weight_in(0, 0)
    multiply(0, 0, 1)
    multiply(0, 1, 0)
    weight_in(1, 0)
    multiply(1, 0, 1)
    multiply(1, 1, 0)
    weight_on(2, 1, 0)
    weight_on(2, 1, 1)
    terms_on(3, 0)
    weight_in(0, 1)
    multiply(0, 1, 1)
    weight_in(2, 0)
    multiply(2, 0, 1)
    weight_in(1, 1)
    multiply(1, 1, 1)
    multiply(2, 1, 0)
    weight_on(3, 1, 0)
    terms_on(3, 1)
    weight_in(3, 0)
    multiply(3, 0, 1)
    weight_in(2, 1)
    multiply(2, 1, 1)
    weight_on(3, 1, 1)
    multiply(3, 1, 0)
    for k in range(DEPTH):
        for plane in range(2):
            s = slot(k, plane, 1)
            landed(terms.at[s], t_recv.at[s])
    kept, width_all = down_grads.shape[0], tags.shape[2]
    marks = tags[0]
    for s in range(1, slots):
        marks = marks + tags[s]
    own_rows = lax.broadcasted_iota(jnp.int32, (kept, width_all), 0) + (me * kept + 1)
    pick = (own_rows == marks[:1]).astype(jnp.bfloat16)
    for kind, grads in ((0, down_grads), (1, up_grads)):
        for c in range(0, grads.shape[1], 512):
            flat = terms[:, kind, :, :, c : c + 512].reshape(width_all, 512)
            grads[:, c : c + 512] = contract(pick, flat, 1, 0)
    weight_in(3, 1)
    multiply(3, 1, 1)
    for j in range(acc.shape[0]):
        out[:, j * CHUNK : (j + 1) * CHUNK] = acc[j].astype(jnp.bfloat16)
    cross.wait_send()
    swap.wait_send()
    for moved, when in started:
        if when is None:
            moved.wait_send()
        else:
            pl.when(when)(moved.wait_send)


def fused_body(
    activations,
    output_gradient,
    levels,
    scales,
    adapter_down_rows,
    adapter_up_rows,
    tenant_per_tile,
    tenant_adapter_index,
):
    rows_dev, inner_local = activations.shape
    in_rows, out_cols = levels.shape
    tiles_here = tenant_per_tile.shape[0]
    held = adapter_down_rows.shape[0] // ADAPTER_RANK
    slots = lax.axis_size("batch")
    adapter_ids = jnp.arange(tenant_adapter_index.shape[0], dtype=jnp.int32)

    def owners(tenants):
        match = (tenants[:, None] == adapter_ids[None, :]).astype(jnp.int32)
        return jnp.sum(match * tenant_adapter_index[None, :], axis=1)

    mine = owners(tenant_per_tile[:, 0])
    spots = jnp.stack([mine // held, mine % held], axis=1)
    terms_here = tiles_here * ADAPTER_RANK
    row_of = jnp.repeat(mine, ADAPTER_RANK) * ADAPTER_RANK + jnp.tile(
        jnp.arange(ADAPTER_RANK, dtype=jnp.int32), tiles_here
    )
    is_mine = jnp.arange(slots, dtype=jnp.int32)[:, None] == lax.axis_index("batch")
    tag = jnp.where(is_mine, row_of[None, :] + 1, 0).reshape(1, slots * terms_here)
    tag = jnp.broadcast_to(tag, (8, slots * terms_here))
    weight_shape = (PIECES, in_rows // PIECES, out_cols)
    factor_shape = (held, ADAPTER_RANK, inner_local)
    vmem = pl.BlockSpec(memory_space=pltpu.VMEM)
    dma = pltpu.SemaphoreType.DMA
    bf16, f32 = jnp.bfloat16, jnp.float32
    return pl.pallas_call(
        fused_kernel,
        out_shape=(
            jax.ShapeDtypeStruct((rows_dev, in_rows), bf16),
            jax.ShapeDtypeStruct((held * ADAPTER_RANK, inner_local), f32),
            jax.ShapeDtypeStruct((held * ADAPTER_RANK, inner_local), f32),
        ),
        in_specs=[pl.BlockSpec(memory_space=pltpu.SMEM)] + [vmem] * 7,
        out_specs=(vmem, vmem, vmem),
        scratch_shapes=[
            pltpu.VMEM(weight_shape, bf16),
            pltpu.VMEM((slots, 2, tiles_here, ADAPTER_RANK, inner_local), bf16),
            pltpu.VMEM((slots,) + tag.shape, jnp.int32),
            pltpu.VMEM((slots,) + weight_shape, bf16),
            pltpu.VMEM((slots, 2) + factor_shape, bf16),
            pltpu.VMEM((2, rows_dev, inner_local), bf16),
            pltpu.VMEM((in_rows // CHUNK, rows_dev, CHUNK), f32),
            pltpu.VMEM((2, rows_dev, 128), f32),
            pltpu.VMEM((2, rows_dev, 128), f32),
            dma((slots, PIECES)),
            dma((2 * DEPTH, PIECES, 4)),
            dma((slots,)),
            dma((2 * DEPTH, 4)),
            dma((slots,)),
            dma((2 * DEPTH, 4)),
            dma((slots,)),
            dma((2 * DEPTH, 4)),
            dma((2,)),
            dma((2,)),
        ],
        compiler_params=pltpu.CompilerParams(
            collective_id=0, has_side_effects=True, vmem_limit_bytes=52 * 2**20
        ),
        cost_estimate=pl.CostEstimate(
            flops=2 * rows_dev * in_rows * out_cols * slots,
            bytes_accessed=2**27,
            transcendentals=0,
        ),
    )(
        spots,
        activations,
        output_gradient,
        levels,
        scales.T,
        adapter_down_rows.reshape(factor_shape),
        adapter_up_rows.reshape(factor_shape),
        tag,
    )


def solution(mesh):
    in_specs = (
        P(("parts", "batch"), "mp"),
        P(("parts", "batch"), "mp"),
        P("mp", "batch"),
        P("mp", "batch"),
        P(("parts", "batch"), "mp"),
        P(("parts", "batch"), "mp"),
        P(("parts", "batch"), None),
        P("parts"),
    )
    out_specs = (
        P(("parts", "batch"), "mp"),
        P(("parts", "batch"), "mp"),
        P(("parts", "batch"), "mp"),
    )
    fused = mesh.shape["batch"] == 16 and mesh.shape["mp"] == 2 and mesh.shape["parts"] == 1
    chosen = fused_body if fused else body
    return jax.shard_map(chosen, mesh=mesh, in_specs=in_specs, out_specs=out_specs, check_vma=False)
```

```python
import jax
import jax.numpy as jnp
from jax import lax
from jax.experimental import pallas as pl
from jax.experimental.pallas import tpu as pltpu
from jax.sharding import PartitionSpec as P

ADAPTER_RANK = 16
QB = 64


def contract(left, right, left_dim, right_dim):
    return lax.dot_general(
        left, right, (((left_dim,), (right_dim,)), ((), ())), preferred_element_type=jnp.float32
    )


def dequantize(level_cols, scale_cols):
    return (
        level_cols.astype(jnp.float32) * jnp.repeat(scale_cols.astype(jnp.float32), QB, axis=1)
    ).astype(jnp.bfloat16)


def body(
    activations,
    output_gradient,
    levels,
    scales,
    adapter_down_rows,
    adapter_up_rows,
    tenant_per_tile,
    tenant_adapter_index,
):
    rows_dev, inner_local = activations.shape
    tiles_here = tenant_per_tile.shape[0]
    tile_rows = rows_dev // tiles_here
    adapter_count = tenant_adapter_index.shape[0]
    full_grads = lax.all_gather(output_gradient, "mp", axis=1, tiled=True)
    local_weight = dequantize(levels, scales)
    base_total = contract(
        full_grads, lax.all_gather(local_weight, "batch", axis=1, tiled=True), 1, 1
    )
    stacked_down_factors, all_up = (
        lax.all_gather(adapter_down_rows, "batch", axis=0, tiled=True),
        lax.all_gather(adapter_up_rows, "batch", axis=0, tiled=True),
    )
    tenants = tenant_per_tile[:, 0]
    adapter_ids = jnp.arange(adapter_count, dtype=jnp.int32)
    tenant_match = (tenants[:, None] == adapter_ids[None, :]).astype(jnp.int32)
    owner_of = jnp.sum(tenant_match * tenant_adapter_index[None, :], axis=1)
    tile_hot = owner_of[:, None] == adapter_ids[None, :]
    row_hot = jnp.broadcast_to(
        tile_hot[:, None, :], (tiles_here, tile_rows, adapter_count)
    ).reshape(rows_dev, adapter_count)
    onehot_float = row_hot.astype(jnp.float32)
    wide_hidden = contract(activations, stacked_down_factors, 1, 1).reshape(
        rows_dev, adapter_count, ADAPTER_RANK
    )
    wide_coeffs = contract(output_gradient, all_up, 1, 1).reshape(
        rows_dev, adapter_count, ADAPTER_RANK
    )
    hidden_share = jnp.sum(wide_hidden * onehot_float[:, :, None], axis=1)
    coefficient_share = jnp.sum(wide_coeffs * onehot_float[:, :, None], axis=1)
    adapter_hidden, adapter_coefficients = (
        lax.psum(hidden_share.astype(jnp.bfloat16), "mp").astype(jnp.float32),
        lax.psum(coefficient_share.astype(jnp.bfloat16), "mp").astype(jnp.float32),
    )
    hidden_narrow16 = adapter_hidden.astype(jnp.bfloat16)
    coefficients16 = adapter_coefficients.astype(jnp.bfloat16)
    hot16 = row_hot.astype(jnp.bfloat16)
    coefficients_widened = (hot16[:, :, None] * coefficients16[:, None, :]).reshape(
        rows_dev, adapter_count * ADAPTER_RANK
    )
    hidden_wide = (hot16[:, :, None] * hidden_narrow16[:, None, :]).reshape(
        rows_dev, adapter_count * ADAPTER_RANK
    )
    adapter_contribution = (
        2.0
        * jnp.dot(coefficients_widened, stacked_down_factors, preferred_element_type=jnp.float32)
    ).astype(jnp.bfloat16)
    down_terms = 2.0 * contract(coefficients_widened, activations, 0, 0)
    up_terms = 2.0 * contract(hidden_wide, output_gradient, 0, 0)
    down_grads, up_grads = (
        lax.psum_scatter(down_terms, "batch", scatter_dimension=0, tiled=True),
        lax.psum_scatter(up_terms, "batch", scatter_dimension=0, tiled=True),
    )
    input_gradient = (base_total + adapter_contribution.astype(jnp.float32)).astype(jnp.bfloat16)
    return (input_gradient, down_grads, up_grads)

DEPTH, PIECES, UP, DOWN, ACROSS, SIBLING = 4, 2, 0, 1, 2, 3
CHUNK = 256


def fused_kernel(
    spots, act, grad, levels, scales_t, down_own, up_own, tag_own,
    out, down_grads, up_grads,
    weight, terms, tags, wbuf, fac, gfull, acc, share, theirs,
    w_recv, w_send, f_recv, f_send, g_recv, g_send, t_recv, t_send, x_recv, x_send,
):
    slots, pieces, piece_rows, width = wbuf.shape
    tiles = spots.shape[0]
    me, half = lax.axis_index("batch"), lax.axis_index("mp")
    z, y, core = me // 4, (me // 2) % 2, me % 2
    place = {
        UP: {"batch": me + 4},
        DOWN: {"batch": me - 4},
        ACROSS: {"batch": z * 4 + (1 - y) * 2 + core},
        SIBLING: {"batch": z * 4 + y * 2 + 1 - core},
    }
    partner = {"mp": 1 - half}
    not_top, not_bottom = z < DEPTH - 1, z > 0

    inner, upper = z * (3 - z) // 2, z // 2

    def near(k):
        v = inner + k - 2 * inner * k if k < 2 else k
        return v + upper * (3 - 2 * v)

    def slot(k, plane, column):
        yy = y if plane == 0 else 1 - y
        cc = core if column == 0 else 1 - core
        return near(k) * 4 + yy * 2 + cc

    barrier = pltpu.get_barrier_semaphore()
    for way, there in ((UP, not_top), (DOWN, not_bottom)):
        @pl.when(there)
        def _(way=way):
            pl.semaphore_signal(barrier, inc=1, device_id=place[way], device_id_type=pl.DeviceIdType.MESH)
    for to in (place[ACROSS], place[SIBLING], partner):
        pl.semaphore_signal(barrier, inc=1, device_id=to, device_id_type=pl.DeviceIdType.MESH)
    pl.semaphore_wait(barrier, 4 + inner)

    started = []

    def copy(src, dst, send, recv, to):
        return pltpu.make_async_remote_copy(
            src_ref=src, dst_ref=dst, send_sem=send, recv_sem=recv,
            device_id=to, device_id_type=pl.DeviceIdType.MESH,
        )

    def push(src, dst, send, recv, way, when=None):
        moved = copy(src, dst, send.at[way], recv, place[way])
        started.append((moved, when))
        if when is None:
            moved.start()
        else:
            pl.when(when)(moved.start)

    def along(src, dst, send, recv, k):
        from_z = near(k)
        push(src, dst, send, recv, UP, jnp.logical_and(from_z <= z, not_top))
        push(src, dst, send, recv, DOWN, jnp.logical_and(from_z >= z, not_bottom))

    def landed(ref, recv):
        copy(ref, ref, x_send.at[0], recv, partner).wait_recv()

    def z_first(ref, own, send, recv, k, plane):
        if k or plane:
            landed(ref, recv)
        src = own if k == 0 and plane == 0 else ref
        if plane == 0:
            along(src, ref, send, recv, k)
            push(src, ref, send, recv, ACROSS)
        push(src, ref, send, recv, SIBLING)

    def y_first(ref, send, recv, k, plane):
        if k or plane:
            landed(ref, recv)
        if k == 0 and plane == 0:
            push(ref, ref, send, recv, ACROSS)
        along(ref, ref, send, recv, k)
        push(ref, ref, send, recv, SIBLING)

    def weight_on(k, plane, p):
        s = slot(k, plane, 0)
        z_first(wbuf.at[s, p], weight.at[p], w_send.at[plane * DEPTH + k, p], w_recv.at[s, p], k, plane)

    def weight_in(k, plane):
        s = slot(k, plane, 1)
        for p in range(pieces):
            landed(wbuf.at[s, p], w_recv.at[s, p])

    def multiply(k, plane, column):
        s = slot(k, plane, column)
        per_half = gfull.shape[2] // width
        cols = pl.ds(pl.multiple_of((s % per_half) * width, width), width)
        own = k == 0 and plane == 0 and column == 0
        per_piece = piece_rows // CHUNK

        @pl.loop(0, pieces * per_piece, unroll=8)
        def _(j):
            rows = pl.ds(pl.multiple_of((j % per_piece) * CHUNK, CHUNK), CHUNK)
            block = weight[j // per_piece, rows, :] if own else wbuf[s, j // per_piece, rows, :]
            acc[j] += contract(gfull[s // per_half, :, cols], block, 1, 1)

    def factor_on(k, plane):
        s = slot(k, plane, 0)
        z_first(fac.at[s], fac.at[s], f_send.at[plane * DEPTH + k], f_recv.at[s], k, plane)
        z_first(tags.at[s], tags.at[s], g_send.at[plane * DEPTH + k], g_recv.at[s], k, plane)

    def terms_on(k, plane):
        s = slot(k, plane, 0)
        y_first(terms.at[s], t_send.at[plane * DEPTH + k], t_recv.at[s], k, plane)

    rank = down_own.shape[1]
    for sub in range(down_own.shape[0]):
        fac[me, 0, sub] = down_own[sub]
        fac[me, 1, sub] = up_own[sub]
    tags[me] = tag_own[...]
    factor_on(0, 0)
    cross = copy(grad, gfull.at[half], x_send.at[0], x_recv.at[0], partner)
    cross.start()

    groups = scales_t.shape[0]
    spread = (
        lax.broadcasted_iota(jnp.int32, (groups, width), 0)
        == lax.broadcasted_iota(jnp.int32, (groups, width), 1) // QB
    ).astype(jnp.bfloat16)

    @pl.loop(0, pieces * piece_rows // CHUNK)
    def _(j):
        rows = pl.ds(pl.multiple_of(j * CHUNK, CHUNK), CHUNK)
        inside = pl.ds(pl.multiple_of((j * CHUNK) % piece_rows, CHUNK), CHUNK)
        factor = contract(scales_t[:, rows], spread, 0, 0)
        weight[j * CHUNK // piece_rows, inside, :] = (
            levels[rows, :].astype(jnp.float32) * factor
        ).astype(jnp.bfloat16)

    gfull[half] = grad[...]
    share[...] = jnp.zeros_like(share)
    factor_on(1, 0)
    factor_on(2, 0)
    weight_on(0, 0, 0)
    factor_on(3, 0)
    weight_on(0, 0, 1)
    weight_on(1, 0, 0)
    weight_on(1, 0, 1)
    for k in range(DEPTH):
        factor_on(k, 1)
    for k in range(DEPTH):
        for plane in range(2):
            s = slot(k, plane, 1)
            landed(fac.at[s], f_recv.at[s])
            landed(tags.at[s], g_recv.at[s])

    tile_rows = act.shape[0] // tiles
    for t in range(tiles):
        rows = pl.ds(t * tile_rows, tile_rows)
        where, sub = spots[t, 0], spots[t, 1]
        share[0, rows, :rank] = contract(act[rows, :], fac[where, 0, sub], 1, 1)
        share[1, rows, :rank] = contract(grad[rows, :], fac[where, 1, sub], 1, 1)
    swap = copy(share, theirs, x_send.at[1], x_recv.at[1], partner)
    swap.start()
    weight_on(2, 0, 0)
    landed(theirs, x_recv.at[1])
    for t in range(tiles):
        rows = pl.ds(t * tile_rows, tile_rows)
        where, sub = spots[t, 0], spots[t, 1]
        hidden = share[0, rows, :] + theirs[0, rows, :]
        coeffs = share[1, rows, :] + theirs[1, rows, :]
        factor = fac[where, 0, sub]
        coeffs16 = coeffs[:, :rank].astype(jnp.bfloat16)
        lora = (2.0 * contract(coeffs16, factor, 1, 0)).astype(jnp.bfloat16).astype(jnp.float32)
        for j in range(acc.shape[0]):
            acc[j, rows, :] = lora[:, j * CHUNK : (j + 1) * CHUNK]
        turned = jnp.transpose(coeffs)[:rank].astype(jnp.bfloat16)
        terms[me, 0, t] = (2.0 * contract(turned, act[rows, :], 1, 0)).astype(jnp.bfloat16)
        turned = jnp.transpose(hidden)[:rank].astype(jnp.bfloat16)
        terms[me, 1, t] = (2.0 * contract(turned, grad[rows, :], 1, 0)).astype(jnp.bfloat16)
    terms_on(0, 0)
    weight_on(2, 0, 1)
    landed(gfull.at[1 - half], x_recv.at[0])
    multiply(0, 0, 0)
    weight_on(3, 0, 0)
    multiply(1, 0, 0)
    weight_on(3, 0, 1)
    terms_on(0, 1)
    terms_on(1, 0)
    terms_on(1, 1)
    weight_on(0, 1, 0)
    weight_on(0, 1, 1)
    terms_on(2, 0)
    multiply(2, 0, 0)
    terms_on(2, 1)
    weight_on(1, 1, 0)
    weight_on(1, 1, 1)
    multiply(3, 0, 0)
    weight_in(0, 0)
    multiply(0, 0, 1)
    multiply(0, 1, 0)
    weight_in(1, 0)
    multiply(1, 0, 1)
    multiply(1, 1, 0)
    weight_on(2, 1, 0)
    weight_on(2, 1, 1)
    terms_on(3, 0)
    weight_in(0, 1)
    multiply(0, 1, 1)
    weight_in(2, 0)
    multiply(2, 0, 1)
    weight_in(1, 1)
    multiply(1, 1, 1)
    multiply(2, 1, 0)
    weight_on(3, 1, 0)
    terms_on(3, 1)
    weight_in(3, 0)
    multiply(3, 0, 1)
    weight_in(2, 1)
    multiply(2, 1, 1)
    weight_on(3, 1, 1)
    multiply(3, 1, 0)
    for k in range(DEPTH):
        for plane in range(2):
            s = slot(k, plane, 1)
            landed(terms.at[s], t_recv.at[s])
    kept, width_all = down_grads.shape[0], tags.shape[2]
    marks = tags[0]
    for s in range(1, slots):
        marks = marks + tags[s]
    own_rows = lax.broadcasted_iota(jnp.int32, (kept, width_all), 0) + (me * kept + 1)
    pick = (own_rows == marks[:1]).astype(jnp.bfloat16)
    for kind, grads in ((0, down_grads), (1, up_grads)):
        for c in range(0, grads.shape[1], 512):
            flat = terms[:, kind, :, :, c : c + 512].reshape(width_all, 512)
            grads[:, c : c + 512] = contract(pick, flat, 1, 0)
    weight_in(3, 1)
    multiply(3, 1, 1)
    for j in range(acc.shape[0]):
        out[:, j * CHUNK : (j + 1) * CHUNK] = acc[j].astype(jnp.bfloat16)
    cross.wait_send()
    swap.wait_send()
    for moved, when in started:
        if when is None:
            moved.wait_send()
        else:
            pl.when(when)(moved.wait_send)


def fused_body(
    activations,
    output_gradient,
    levels,
    scales,
    adapter_down_rows,
    adapter_up_rows,
    tenant_per_tile,
    tenant_adapter_index,
):
    rows_dev, inner_local = activations.shape
    in_rows, out_cols = levels.shape
    tiles_here = tenant_per_tile.shape[0]
    held = adapter_down_rows.shape[0] // ADAPTER_RANK
    slots = lax.axis_size("batch")
    adapter_ids = jnp.arange(tenant_adapter_index.shape[0], dtype=jnp.int32)

    def owners(tenants):
        match = (tenants[:, None] == adapter_ids[None, :]).astype(jnp.int32)
        return jnp.sum(match * tenant_adapter_index[None, :], axis=1)

    mine = owners(tenant_per_tile[:, 0])
    spots = jnp.stack([mine // held, mine % held], axis=1)
    terms_here = tiles_here * ADAPTER_RANK
    row_of = jnp.repeat(mine, ADAPTER_RANK) * ADAPTER_RANK + jnp.tile(
        jnp.arange(ADAPTER_RANK, dtype=jnp.int32), tiles_here
    )
    is_mine = jnp.arange(slots, dtype=jnp.int32)[:, None] == lax.axis_index("batch")
    tag = jnp.where(is_mine, row_of[None, :] + 1, 0).reshape(1, slots * terms_here)
    tag = jnp.broadcast_to(tag, (8, slots * terms_here))
    weight_shape = (PIECES, in_rows // PIECES, out_cols)
    factor_shape = (held, ADAPTER_RANK, inner_local)
    vmem = pl.BlockSpec(memory_space=pltpu.VMEM)
    dma = pltpu.SemaphoreType.DMA
    bf16, f32 = jnp.bfloat16, jnp.float32
    return pl.pallas_call(
        fused_kernel,
        out_shape=(
            jax.ShapeDtypeStruct((rows_dev, in_rows), bf16),
            jax.ShapeDtypeStruct((held * ADAPTER_RANK, inner_local), f32),
            jax.ShapeDtypeStruct((held * ADAPTER_RANK, inner_local), f32),
        ),
        in_specs=[pl.BlockSpec(memory_space=pltpu.SMEM)] + [vmem] * 7,
        out_specs=(vmem, vmem, vmem),
        scratch_shapes=[
            pltpu.VMEM(weight_shape, bf16),
            pltpu.VMEM((slots, 2, tiles_here, ADAPTER_RANK, inner_local), bf16),
            pltpu.VMEM((slots,) + tag.shape, jnp.int32),
            pltpu.VMEM((slots,) + weight_shape, bf16),
            pltpu.VMEM((slots, 2) + factor_shape, bf16),
            pltpu.VMEM((2, rows_dev, inner_local), bf16),
            pltpu.VMEM((in_rows // CHUNK, rows_dev, CHUNK), f32),
            pltpu.VMEM((2, rows_dev, 128), f32),
            pltpu.VMEM((2, rows_dev, 128), f32),
            dma((slots, PIECES)),
            dma((2 * DEPTH, PIECES, 4)),
            dma((slots,)),
            dma((2 * DEPTH, 4)),
            dma((slots,)),
            dma((2 * DEPTH, 4)),
            dma((slots,)),
            dma((2 * DEPTH, 4)),
            dma((2,)),
            dma((2,)),
        ],
        compiler_params=pltpu.CompilerParams(
            collective_id=0, has_side_effects=True, vmem_limit_bytes=52 * 2**20
        ),
        cost_estimate=pl.CostEstimate(
            flops=2 * rows_dev * in_rows * out_cols * slots,
            bytes_accessed=2**27,
            transcendentals=0,
        ),
    )(
        spots,
        activations,
        output_gradient,
        levels,
        scales.T,
        adapter_down_rows.reshape(factor_shape),
        adapter_up_rows.reshape(factor_shape),
        tag,
    )


def solution(mesh):
    in_specs = (
        P(("parts", "batch"), "mp"),
        P(("parts", "batch"), "mp"),
        P("mp", "batch"),
        P("mp", "batch"),
        P(("parts", "batch"), "mp"),
        P(("parts", "batch"), "mp"),
        P(("parts", "batch"), None),
        P("parts"),
    )
    out_specs = (
        P(("parts", "batch"), "mp"),
        P(("parts", "batch"), "mp"),
        P(("parts", "batch"), "mp"),
    )
    fused = mesh.shape["batch"] == 16 and mesh.shape["mp"] == 2 and mesh.shape["parts"] == 1
    chosen = fused_body if fused else body
    return jax.shard_map(chosen, mesh=mesh, in_specs=in_specs, out_specs=out_specs, check_vma=False)
```
